32 devices in a mesh: leaf: 4 (over x, core), row: 2 (over y), col: 4 (over z).
Axes of the slice: x: 2, y: 2, z: 4, core: 2. Of those that a mesh axis runs over, the one named last changes fastest.
Arguments:
- child_front: float32 [4, 4096, 4096], P('leaf', 'row', 'col'), as said below
- parent_front: bfloat16 [8192, 16384], P('row', ('leaf', 'col')), as said below
- block_map: int32 [4, 28], replicated, may hold values from 0 to 63, as said below
Outputs:
- child_panel_t: float32 [4, 512, 4096], P('leaf', 'col', 'row')
- parent_panel_t: float32 [1024, 8192], P(('leaf', 'col'), 'row')
- parent_update: float32 [8192, 16384], P('row', ('leaf', 'col'))
The draws below stay inside these ranges and needn't reach their ends.
Inputs may be any that keep to these rules, and one draw needn't show every extreme that they name: `child_front`: every child front is symmetric positive definite. `parent_front`: every parent front (each block of 8192 columns) is symmetric positive definite. `block_map`: in each row the entries are distinct. Of the contribution blocks that one device of a child's grid holds in its rows, at most 8 go to parent blocks whose rows one index of row holds; of those it holds in its columns, at most 2 go to parent blocks whose columns are held by one index of col, counting both leaves of the pair together; of all contribution blocks of one child, at most 14 go to parent blocks whose rows one index of row holds. All three bounds are reached.
All inputs are finite; a program needn't handle non-finite values.
Results may differ from the reference program's by a relative error of at most 0.0003.
Values sent between devices are 32-bit elements; how exact they have to be, the bound alone decides.
A program may use at most 192 MiB of HBM per device.

```python
import jax
import jax.numpy as jnp
from jax import lax

NC = 4096
NP = 8192
BLK = 128
PBC = 512
PBP = 512
CB = 28
PRB = 64
PARENT_COL_BLOCKS = 8
PARENTS = 2
N_LEAF = 4
N_ROW = 2
N_COL = 4


def symmetric_stack(key, copies, order):
    shape = (copies, order, order)
    random_part = jnp.clip(jax.random.normal(key, shape, jnp.float32), -4.0, 4.0)
    symmetric = (random_part + jnp.swapaxes(random_part, 1, 2)) * (0.7071 * order ** (-0.25))
    diagonal = jax.random.uniform(jax.random.fold_in(key, 7), (copies, order, 1), jnp.float32, 2.3, 3.0) * order ** 0.25
    on_diagonal = jnp.arange(order)[:, None] == jnp.arange(order)[None, :]
    return jnp.where(on_diagonal[None], diagonal, symmetric)


def draw_child_front(key, part):
    return symmetric_stack(key, N_LEAF, NC)


def draw_parent_front(key, part):
    stacked = symmetric_stack(key, PARENTS, NP)
    return jnp.transpose(stacked, (1, 0, 2)).reshape(NP, PARENTS * NP).astype(jnp.bfloat16)


def draw_block_map(key, part):
    slope = 2 * N_COL // N_ROW
    block_ids = jnp.arange(CB)
    shift = jax.random.randint(jax.random.fold_in(key, 11), (N_LEAF, 1), 0, 2 * N_COL)
    holding_device = ((slope * block_ids + slope * block_ids // (2 * N_COL))[None, :] + shift) % (2 * N_COL)
    same_owner = holding_device[:, :, None] == holding_device[:, None, :]
    earlier = block_ids[None, :] < block_ids[:, None]
    device_number = jnp.sum(same_owner & earlier[None], axis=2)
    start_positions = jax.random.randint(jax.random.fold_in(key, 13), (N_LEAF, 2 * N_COL), 0, PARENT_COL_BLOCKS)
    selected_entries = jnp.sum(start_positions[:, None, :] * (holding_device[:, :, None] == jnp.arange(2 * N_COL)[None, None, :]), axis=2)
    return (holding_device * PARENT_COL_BLOCKS + (device_number + selected_entries) % PARENT_COL_BLOCKS).astype(jnp.int32)


def setup_inputs(seed: int = 0) -> dict:
    seeds = jax.random.split(jax.random.key(seed), 4)
    return {
        "child_front": draw_child_front(jax.random.fold_in(seeds[3], 71), 0),
        "parent_front": draw_parent_front(jax.random.fold_in(seeds[3], 71), 0),
        "block_map": draw_block_map(jax.random.fold_in(seeds[3], 71), 0),
    }


def factor(front_matrix, panel_width):
    lower_factor = jnp.linalg.cholesky(front_matrix[:panel_width, :panel_width])
    panel_factor = jax.scipy.linalg.solve_triangular(lower_factor, front_matrix[:, :panel_width].T, lower=True).T
    update = jnp.dot(panel_factor, panel_factor.T, precision=lax.Precision.HIGHEST)
    index_ids = jnp.arange(front_matrix.shape[0])
    keep_mask = (index_ids[:, None] >= panel_width) & (index_ids[None, :] >= panel_width)
    return (panel_factor, jnp.where(keep_mask, front_matrix - update, jnp.float32(0.0)))

def reference(child_front, parent_front, block_map):
    child_panels = []
    tile_sets = []
    for child in range(N_LEAF):
        panel_factor, schur_part = factor(child_front[child], PBC)
        child_panels.append(panel_factor.T)
        blocks = schur_part[PBC:, PBC:].reshape(CB, BLK, CB, BLK).transpose(0, 2, 1, 3)
        tile_sets.append(blocks)
    parent_panels = []
    updates = []
    for parent in range(PARENTS):
        front_matrix = parent_front[:, parent * NP:(parent + 1) * NP].astype(jnp.float32)
        tile_grid = front_matrix.reshape(PRB, BLK, PRB, BLK).transpose(0, 2, 1, 3)
        for child in (2 * parent, 2 * parent + 1):
            mapping = block_map[child].astype(jnp.int32)
            tile_grid = tile_grid.at[mapping[:, None], mapping[None, :]].add(tile_sets[child])
        assembled = tile_grid.transpose(0, 2, 1, 3).reshape(NP, NP)
        panel_factor, schur_part = factor(assembled, PBP)
        parent_panels.append(panel_factor.T)
        updates.append(schur_part)
    return (jnp.stack(child_panels), jnp.concatenate(parent_panels, axis=0), jnp.concatenate(updates, axis=1))
```

```python
import functools

import jax
import jax.numpy as jnp
from jax import lax
from jax.experimental import pallas as pl
from jax.experimental.pallas import tpu as pltpu
from jax.sharding import PartitionSpec as P

BLK = 128
HIGH = lax.Precision.HIGH
HIGHEST = lax.Precision.HIGHEST
VMEM_BYTES = 40 * 1024 * 1024


def from_root(value, axes, is_root):
    return lax.psum(jnp.where(is_root, value, jnp.zeros_like(value)), axes)


def pair_swap(value):
    pairs = [(source, source ^ 1) for source in range(lax.axis_size("leaf"))]
    return lax.ppermute(value, "leaf", pairs)


def shift_rows(value, step):
    count = lax.axis_size("row")
    return lax.ppermute(value, "row", [(s, (s + step) % count) for s in range(count)])


def params():
    return pltpu.CompilerParams(vmem_limit_bytes=VMEM_BYTES)


def eliminate_block(block):
    groups = [block[8 * g : 8 * g + 8, :] for g in range(BLK // 8)]
    lanes = lax.broadcasted_iota(jnp.int32, (1, BLK), 1)
    subs = lax.broadcasted_iota(jnp.int32, (8, 1), 0)
    for j in range(BLK):
        first, sub = j // 8, j % 8
        pivot_row = groups[first][sub : sub + 1, :]
        pivot = pivot_row[:, j : j + 1]
        scaled = jnp.where(lanes == j, pivot + 1.0, pivot_row) / pivot
        for g in range(first, BLK // 8):
            column = groups[g][:, j : j + 1]
            if g == first:
                if sub == 7:
                    continue
                column = jnp.where(subs > sub, column, 0.0)
            groups[g] = groups[g] - column * scaled
    full = jnp.concatenate(groups, axis=0)
    rows = lax.broadcasted_iota(jnp.int32, (BLK, BLK), 0)
    cols = lax.broadcasted_iota(jnp.int32, (BLK, BLK), 1)
    diagonal = jnp.sum(jnp.where(rows == cols, full, 0.0), axis=1, keepdims=True)
    unit = jnp.where(rows == cols, 1.0, jnp.where(cols < rows, full, 0.0))
    return unit * lax.rsqrt(diagonal)


def inverse_kernel(block_ref, out_ref, work):
    width = block_ref.shape[0]
    count = width // BLK
    work[...] = block_ref[...]
    row_ids = lax.broadcasted_iota(jnp.int32, (width, width), 0)
    col_ids = lax.broadcasted_iota(jnp.int32, (width, width), 1)
    out_ref[...] = jnp.where(row_ids == col_ids, 1.0, 0.0).astype(jnp.float32)
    for k in range(count):
        low, high = k * BLK, (k + 1) * BLK
        small = eliminate_block(work[low:high, low:high])
        out_ref[low:high, :high] = jnp.dot(
            small, out_ref[low:high, :high], precision=HIGHEST, preferred_element_type=jnp.float32
        )
        if high == width:
            continue
        upper = jnp.dot(
            small, work[low:high, high:], precision=HIGHEST, preferred_element_type=jnp.float32
        )
        lower = upper.T
        work[high:, high:] = work[high:, high:] - jnp.dot(
            lower, upper, precision=HIGHEST, preferred_element_type=jnp.float32
        )
        out_ref[high:, :high] = out_ref[high:, :high] - jnp.dot(
            lower, out_ref[low:high, :high], precision=HIGHEST, preferred_element_type=jnp.float32
        )


def inverse_factor_of(diagonal_block):
    width = diagonal_block.shape[0]
    return pl.pallas_call(
        inverse_kernel,
        out_shape=jax.ShapeDtypeStruct((width, width), jnp.float32),
        in_specs=[pl.BlockSpec(memory_space=pltpu.VMEM)],
        out_specs=pl.BlockSpec(memory_space=pltpu.VMEM),
        scratch_shapes=[pltpu.VMEM((width, width), jnp.float32)],
        compiler_params=params(),
        cost_estimate=pl.CostEstimate(
            flops=60_000_000_000, bytes_accessed=width * width * 8, transcendentals=0
        ),
        name="inverse_factor",
    )(diagonal_block)


def split_parts(value):
    head = value.astype(jnp.bfloat16)
    tail = (value - head.astype(jnp.float32)).astype(jnp.bfloat16)
    return head, tail


def three_dots(rows, cols_head, cols_tail):
    head, tail = split_parts(rows)
    dot = functools.partial(jnp.dot, preferred_element_type=jnp.float32)
    return dot(head, cols_head) + (dot(head, cols_tail) + dot(tail, cols_head))


def child_schur_kernel(
    row_pick, col_pick, front_ref, rows_ref, cols_ref, out_ref, cols_head, cols_tail, schur
):
    @pl.when((pl.program_id(0) == 0) & (pl.program_id(1) == 0))
    def _():
        cols_head[...], cols_tail[...] = split_parts(cols_ref[...])

    schur[...] = front_ref[...] - three_dots(rows_ref[...], cols_head[...], cols_tail[...])
    cap_cols = out_ref.shape[1]
    for j in range(cap_cols):
        for e in range(out_ref.shape[4] // BLK):
            start = pl.multiple_of(col_pick[e * cap_cols + j] * BLK, BLK)
            out_ref[0, j, 0, :, e * BLK : (e + 1) * BLK] = schur[:, pl.ds(start, BLK)]


def child_strips(front, rows_factor, cols_factor, row_pick, col_pick):
    row_count, cap_rows = row_pick.shape
    col_count, cap_cols = col_pick.shape
    width, cols = cols_factor.shape
    grid_spec = pltpu.PrefetchScalarGridSpec(
        num_scalar_prefetch=2,
        grid=(row_count, cap_rows),
        in_specs=[
            pl.BlockSpec((BLK, cols), lambda t, a, rp, cp: (rp[t * cap_rows + a], 0)),
            pl.BlockSpec((BLK, width), lambda t, a, rp, cp: (rp[t * cap_rows + a], 0)),
            pl.BlockSpec((width, cols), lambda t, a, rp, cp: (0, 0)),
        ],
        out_specs=pl.BlockSpec(
            (1, cap_cols, 1, BLK, col_count * BLK), lambda t, a, rp, cp: (t, 0, a, 0, 0)
        ),
        scratch_shapes=[
            pltpu.VMEM((width, cols), jnp.bfloat16),
            pltpu.VMEM((width, cols), jnp.bfloat16),
            pltpu.VMEM((BLK, cols), jnp.float32),
        ],
    )
    return pl.pallas_call(
        child_schur_kernel,
        grid_spec=grid_spec,
        out_shape=jax.ShapeDtypeStruct(
            (row_count, cap_cols, cap_rows, BLK, col_count * BLK), jnp.float32
        ),
        compiler_params=params(),
        name="child_schur",
    )(row_pick.reshape(-1), col_pick.reshape(-1), front, rows_factor, cols_factor)


def parent_schur_kernel(starts, front_ref, rows_ref, cols_ref, out_ref, cols_head, cols_tail):
    step = pl.program_id(0)

    @pl.when(step == 0)
    def _():
        cols_head[...], cols_tail[...] = split_parts(cols_ref[...])

    width = cols_ref.shape[0]
    shape = out_ref.shape
    row_ids = starts[0] + step * shape[0] + lax.broadcasted_iota(jnp.int32, (shape[0], 1), 0)
    col_ids = starts[1] + lax.broadcasted_iota(jnp.int32, (1, shape[1]), 1)
    update = three_dots(rows_ref[...], cols_head[...], cols_tail[...])
    keep = (row_ids >= width) & (col_ids >= width)
    out_ref[...] = jnp.where(keep, front_ref[...] - update, 0.0)


def parent_schur_of(front, rows_factor, cols_factor, starts):
    rows, cols = front.shape
    width = cols_factor.shape[0]
    tile = 2 * BLK
    grid_spec = pltpu.PrefetchScalarGridSpec(
        num_scalar_prefetch=1,
        grid=(rows // tile,),
        in_specs=[
            pl.BlockSpec((tile, cols), lambda i, s: (i, 0)),
            pl.BlockSpec((tile, width), lambda i, s: (i, 0)),
            pl.BlockSpec((width, cols), lambda i, s: (0, 0)),
        ],
        out_specs=pl.BlockSpec((tile, cols), lambda i, s: (i, 0)),
        scratch_shapes=[
            pltpu.VMEM((width, cols), jnp.bfloat16),
            pltpu.VMEM((width, cols), jnp.bfloat16),
        ],
    )
    return pl.pallas_call(
        parent_schur_kernel,
        grid_spec=grid_spec,
        out_shape=jax.ShapeDtypeStruct((rows, cols), jnp.float32),
        compiler_params=params(),
        name="parent_schur",
    )(starts, front, rows_factor, cols_factor)


def squeeze_kernel(source, *refs):
    ins, out_ref = refs[:-1], refs[-1]
    step = pl.program_id(0)
    for t, ref in enumerate(ins):

        @pl.when(source[2 * step] == t)
        def _(ref=ref):
            for e in range(out_ref.shape[0]):
                out_ref[e, 0] = ref[0, :, e * BLK : (e + 1) * BLK]


def squeeze_rows(parts, source):
    incoming = source.shape[0]
    cols = parts[0].shape[2]
    count = cols // BLK
    grid_spec = pltpu.PrefetchScalarGridSpec(
        num_scalar_prefetch=1,
        grid=(incoming,),
        in_specs=[pl.BlockSpec((1, BLK, cols), lambda m, s: (s[2 * m + 1], 0, 0)) for _ in parts],
        out_specs=pl.BlockSpec((count, 1, BLK, BLK), lambda m, s: (0, m, 0, 0)),
    )
    return pl.pallas_call(
        squeeze_kernel,
        grid_spec=grid_spec,
        out_shape=jax.ShapeDtypeStruct((count, incoming, BLK, BLK), jnp.float32),
        compiler_params=params(),
        name="squeeze_rows",
    )(source.reshape(-1), *parts)


def extend_add_kernel(cap_cols, row_from, col_from, front_ref, *refs):
    pieces, out_ref = refs[:-1], refs[-1]
    step = pl.program_id(0)
    span = out_ref.shape[1] // BLK
    for y in range(span):
        lanes = slice(y * BLK, (y + 1) * BLK)
        total = front_ref[:, lanes].astype(jnp.float32)
        for child in range(2):
            valid_row = row_from[child * pl.num_programs(0) + step] >= 0
            for j in range(cap_cols):
                place = col_from[(child * cap_cols + j) * span + y]
                tile = pieces[child * cap_cols + j][jnp.maximum(place, 0), 0]
                total = total + jnp.where(valid_row & (place >= 0), tile, 0.0)
        out_ref[:, lanes] = total


def extend_add(front, pieces, row_from, col_from):
    rows, cols = front.shape
    cap_cols = col_from.shape[1]
    blocks = rows // BLK
    count = pieces[0].shape[0]

    def piece_spec(child):
        return pl.BlockSpec(
            (count, 1, BLK, BLK),
            lambda x, rf, cf: (0, jnp.maximum(rf[child * blocks + x], 0), 0, 0),
        )

    grid_spec = pltpu.PrefetchScalarGridSpec(
        num_scalar_prefetch=2,
        grid=(blocks,),
        in_specs=[pl.BlockSpec((BLK, cols), lambda x, rf, cf: (x, 0))]
        + [piece_spec(child) for child in range(2) for _ in range(cap_cols)],
        out_specs=pl.BlockSpec((BLK, cols), lambda x, rf, cf: (x, 0)),
    )
    return pl.pallas_call(
        functools.partial(extend_add_kernel, cap_cols),
        grid_spec=grid_spec,
        out_shape=jax.ShapeDtypeStruct((rows, cols), jnp.float32),
        compiler_params=params(),
        name="extend_add",
    )(row_from.reshape(-1), col_from.reshape(-1), front, *pieces)


def find(match, values, missing):
    found = jnp.sum(jnp.where(match, values, 0), axis=-1)
    return jnp.where(jnp.any(match, axis=-1), found, missing).astype(jnp.int32)


def ranks(group):
    ids = jnp.arange(group.shape[0])
    earlier = ids[None, :] < ids[:, None]
    return jnp.sum(earlier & (group[None, :] == group[:, None]), axis=1)


def shards(child_front, parent_front, block_map):
    leaf_id = lax.axis_index("leaf")
    row_id = lax.axis_index("row")
    col_id = lax.axis_index("col")
    row_count = lax.axis_size("row")
    col_count = lax.axis_size("col")
    own_half = leaf_id % 2

    child_block = child_front[0]
    child_rows, child_cols = child_block.shape
    width = child_cols // 2
    at_corner = (row_id == 0) & (col_id == 0)
    diagonal = from_root(child_block[:width, :width], ("row", "col"), at_corner)
    child_block, diagonal = lax.optimization_barrier((child_block, diagonal))
    slab = from_root(child_block[:, :width], "col", col_id == 0)
    top = from_root(child_block[:width], "row", row_id == 0)
    inverse = inverse_factor_of(diagonal)
    cols_factor = jnp.dot(inverse, top, precision=HIGH)
    rows_factor = jnp.dot(slab, inverse.T, precision=HIGH)
    out_width = width // col_count
    inverse_share = lax.dynamic_slice_in_dim(inverse, col_id * out_width, out_width, 0)
    child_out = lax.dot_general(inverse_share, slab, (((1,), (1,)), ((), ())), precision=HIGH)[None]

    parent_rows, parent_cols = parent_front.shape
    parent_order = parent_rows * row_count
    row_span = parent_rows // BLK
    col_span = parent_cols // BLK
    cap_rows = max(1, child_rows // BLK // row_count)
    cap_cols = max(1, child_cols // BLK // col_count)
    block_count = block_map.shape[1]
    cap_incoming = -(-block_count // row_count)
    global_ids = width + jnp.arange(block_count) * BLK
    src_row = global_ids // child_rows
    src_col = global_ids // child_cols

    def routes(mapping):
        dst_row = mapping // row_span
        owner = mapping // col_span
        rank_row = ranks(src_row * row_count + dst_row)
        rank_col = ranks(src_col * col_count + owner % col_count)
        return dst_row, owner, rank_row, rank_col, ranks(dst_row)

    own_map = lax.dynamic_index_in_dim(block_map, leaf_id, 0, keepdims=False)
    pair_map = lax.dynamic_index_in_dim(block_map, leaf_id ^ 1, 0, keepdims=False)
    dst_row, owner, rank_row, rank_col, rank_dest = routes(own_map)
    distance = jnp.arange(row_count)[:, None, None]
    row_pick = find(
        (src_row == row_id)
        & (dst_row == (row_id + distance) % row_count)
        & (rank_row == jnp.arange(cap_rows)[None, :, None]),
        (global_ids - row_id * child_rows) // BLK,
        0,
    )
    col_pick = find(
        (src_col == col_id)
        & (owner % col_count == jnp.arange(col_count)[:, None, None])
        & (rank_col == jnp.arange(cap_cols)[None, :, None]),
        (global_ids - col_id * child_cols) // BLK,
        0,
    )
    incoming = (dst_row == row_id) & (rank_dest == jnp.arange(cap_incoming)[:, None])
    source = jnp.stack(
        [find(incoming, (row_id - src_row) % row_count, 0), find(incoming, rank_row, 0)], axis=1
    )
    row_from, col_from = [], []
    for mapping in (own_map, pair_map):
        to_row, to_owner, _, to_rank_col, to_rank_dest = routes(mapping)
        row_from.append(
            find(
                (to_row == row_id) & (mapping % row_span == jnp.arange(row_span)[:, None]),
                to_rank_dest,
                -1,
            )
        )
        col_from.append(
            find(
                (to_owner == own_half * col_count + col_id)
                & (mapping % col_span == jnp.arange(col_span)[:, None])
                & (to_rank_col == jnp.arange(cap_cols)[:, None, None]),
                src_col,
                -1,
            )
        )
    row_from = jnp.stack(row_from)
    col_from = jnp.stack(col_from)

    strips = child_strips(child_block, rows_factor, cols_factor, row_pick, col_pick)
    own_pieces, pair_pieces = [], []
    for j in range(cap_cols):
        parts = [strips[0, j]] + [shift_rows(strips[t, j], t) for t in range(1, row_count)]
        sending = squeeze_rows(parts, source)
        landed = lax.all_to_all(
            sending.reshape(col_count, cap_incoming * BLK, BLK),
            "col",
            split_axis=0,
            concat_axis=0,
            tiled=True,
        ).reshape(col_count, cap_incoming, BLK, BLK)
        own_pieces.append(landed)
        pair_pieces.append(pair_swap(landed))
    assembled = extend_add(parent_front, own_pieces + pair_pieces, row_from, col_from)

    parent_width = parent_cols // 2
    corner = from_root(
        assembled[:parent_width, :parent_width], ("row", "col"), at_corner
    )
    corner = jnp.where(own_half == 0, corner, pair_swap(corner))
    strip, corner = lax.optimization_barrier((assembled[:parent_width], corner))
    parent_top = from_root(strip, "row", row_id == 0)
    if row_count == 2:
        part = parent_width // 2
        kept = jnp.where(own_half == 0, parent_top[:part], parent_top[part:])
        given = jnp.where(own_half == 0, parent_top[part:], parent_top[:part])
        kept = jnp.where(own_half == row_id, kept, pair_swap(given))
        gathered = lax.all_gather(kept, "col")
        other = pair_swap(gathered)
        first = jnp.where(own_half == 0, gathered, other)
        second = jnp.where(own_half == 0, other, gathered)
        panel_t = jnp.concatenate((first, second), axis=1)
    else:
        panel = from_root(assembled[:, :parent_width], "col", col_id == 0)
        panel = jnp.where(own_half == 0, panel, pair_swap(panel))
        panel_t = panel.T[None]
    parent_inverse = inverse_factor_of(corner)
    parent_cols_factor = jnp.dot(parent_inverse, parent_top, precision=HIGH)
    parent_rows_factor = jnp.einsum("cks,pk->csp", panel_t, parent_inverse, precision=HIGH)
    parent_rows_factor = parent_rows_factor.reshape(parent_rows, parent_width)
    share_width = parent_width // (2 * col_count)
    share_start = (own_half * col_count + col_id) * share_width
    share = lax.dynamic_slice_in_dim(parent_inverse, share_start, share_width, 0)
    parent_out = jnp.einsum("qk,cks->qcs", share, panel_t, precision=HIGH)
    parent_out = parent_out.reshape(share_width, parent_rows)
    col_start = own_half * (parent_order // 2) + col_id * parent_cols
    starts = jnp.stack([row_id * parent_rows, col_start]).astype(jnp.int32)
    parent_schur = parent_schur_of(assembled, parent_rows_factor, parent_cols_factor, starts)
    return (child_out, parent_out, parent_schur)


def solution(mesh):
    placed = (P("leaf", "row", "col"), P("row", ("leaf", "col")), P())
    return jax.shard_map(
        shards,
        mesh=mesh,
        in_specs=placed,
        out_specs=(P("leaf", "col", "row"), P(("leaf", "col"), "row"), P("row", ("leaf", "col"))),
        check_vma=False,
    )
```

```python
import functools

import jax
import jax.numpy as jnp
from jax import lax
from jax.experimental import pallas as pl
from jax.experimental.pallas import tpu as pltpu
from jax.sharding import PartitionSpec as P

BLK = 128
HIGH = lax.Precision.HIGH
HIGHEST = lax.Precision.HIGHEST
VMEM_BYTES = 40 * 1024 * 1024


def from_root(value, axes, is_root):
    return lax.psum(jnp.where(is_root, value, jnp.zeros_like(value)), axes)


def pair_swap(value):
    pairs = [(source, source ^ 1) for source in range(lax.axis_size("leaf"))]
    return lax.ppermute(value, "leaf", pairs)


def shift_rows(value, step):
    count = lax.axis_size("row")
    return lax.ppermute(value, "row", [(s, (s + step) % count) for s in range(count)])


def from_first_row(value):
    at_first = lax.axis_index("row") == 0
    if lax.axis_size("row") != 2:
        return from_root(value, "row", at_first)
    return jnp.where(at_first, value, lax.ppermute(value, "row", [(0, 1)]))


def params():
    return pltpu.CompilerParams(vmem_limit_bytes=VMEM_BYTES)


def eliminate_block(block):
    groups = [block[8 * g : 8 * g + 8, :] for g in range(BLK // 8)]
    lanes = lax.broadcasted_iota(jnp.int32, (1, BLK), 1)
    subs = lax.broadcasted_iota(jnp.int32, (8, 1), 0)
    for j in range(BLK):
        first, sub = j // 8, j % 8
        pivot_row = groups[first][sub : sub + 1, :]
        pivot = pivot_row[:, j : j + 1]
        scaled = jnp.where(lanes == j, pivot + 1.0, pivot_row) / pivot
        for g in range(first, BLK // 8):
            column = groups[g][:, j : j + 1]
            if g == first:
                if sub == 7:
                    continue
                column = jnp.where(subs > sub, column, 0.0)
            groups[g] = groups[g] - column * scaled
    full = jnp.concatenate(groups, axis=0)
    rows = lax.broadcasted_iota(jnp.int32, (BLK, BLK), 0)
    cols = lax.broadcasted_iota(jnp.int32, (BLK, BLK), 1)
    diagonal = jnp.sum(jnp.where(rows == cols, full, 0.0), axis=1, keepdims=True)
    unit = jnp.where(rows == cols, 1.0, jnp.where(cols < rows, full, 0.0))
    return unit * lax.rsqrt(diagonal)


def inverse_kernel(block_ref, out_ref, work):
    width = block_ref.shape[0]
    count = width // BLK
    work[...] = block_ref[...]
    row_ids = lax.broadcasted_iota(jnp.int32, (width, width), 0)
    col_ids = lax.broadcasted_iota(jnp.int32, (width, width), 1)
    out_ref[...] = jnp.where(row_ids == col_ids, 1.0, 0.0).astype(jnp.float32)
    for k in range(count):
        low, high = k * BLK, (k + 1) * BLK
        small = eliminate_block(work[low:high, low:high])
        out_ref[low:high, :high] = jnp.dot(
            small, out_ref[low:high, :high], precision=HIGHEST, preferred_element_type=jnp.float32
        )
        if high == width:
            continue
        upper = jnp.dot(
            small, work[low:high, high:], precision=HIGHEST, preferred_element_type=jnp.float32
        )
        lower = upper.T
        work[high:, high:] = work[high:, high:] - jnp.dot(
            lower, upper, precision=HIGHEST, preferred_element_type=jnp.float32
        )
        out_ref[high:, :high] = out_ref[high:, :high] - jnp.dot(
            lower, out_ref[low:high, :high], precision=HIGHEST, preferred_element_type=jnp.float32
        )


def inverse_factor_of(diagonal_block):
    width = diagonal_block.shape[0]
    return pl.pallas_call(
        inverse_kernel,
        out_shape=jax.ShapeDtypeStruct((width, width), jnp.float32),
        in_specs=[pl.BlockSpec(memory_space=pltpu.VMEM)],
        out_specs=pl.BlockSpec(memory_space=pltpu.VMEM),
        scratch_shapes=[pltpu.VMEM((width, width), jnp.float32)],
        compiler_params=params(),
        cost_estimate=pl.CostEstimate(
            flops=60_000_000_000, bytes_accessed=width * width * 8, transcendentals=0
        ),
        name="inverse_factor",
    )(diagonal_block)


def split_parts(value):
    head = value.astype(jnp.bfloat16)
    tail = (value - head.astype(jnp.float32)).astype(jnp.bfloat16)
    return head, tail


def three_dots(rows, cols_head, cols_tail):
    head, tail = split_parts(rows)
    dot = functools.partial(jnp.dot, preferred_element_type=jnp.float32)
    return dot(head, cols_head) + (dot(head, cols_tail) + dot(tail, cols_head))


def child_schur_kernel(
    row_pick, col_pick, front_ref, rows_ref, cols_ref, out_ref, cols_head, cols_tail, schur
):
    @pl.when((pl.program_id(0) == 0) & (pl.program_id(1) == 0))
    def _():
        cols_head[...], cols_tail[...] = split_parts(cols_ref[...])

    schur[...] = front_ref[...] - three_dots(rows_ref[...], cols_head[...], cols_tail[...])
    cap_cols = out_ref.shape[1]
    for j in range(cap_cols):
        for e in range(out_ref.shape[4] // BLK):
            start = pl.multiple_of(col_pick[e * cap_cols + j] * BLK, BLK)
            out_ref[0, j, 0, :, e * BLK : (e + 1) * BLK] = schur[:, pl.ds(start, BLK)]


def child_strips(front, rows_factor, cols_factor, row_pick, col_pick):
    row_count, cap_rows = row_pick.shape
    col_count, cap_cols = col_pick.shape
    width, cols = cols_factor.shape
    grid_spec = pltpu.PrefetchScalarGridSpec(
        num_scalar_prefetch=2,
        grid=(row_count, cap_rows),
        in_specs=[
            pl.BlockSpec((BLK, cols), lambda t, a, rp, cp: (rp[t * cap_rows + a], 0)),
            pl.BlockSpec((BLK, width), lambda t, a, rp, cp: (rp[t * cap_rows + a], 0)),
            pl.BlockSpec((width, cols), lambda t, a, rp, cp: (0, 0)),
        ],
        out_specs=pl.BlockSpec(
            (1, cap_cols, 1, BLK, col_count * BLK), lambda t, a, rp, cp: (t, 0, a, 0, 0)
        ),
        scratch_shapes=[
            pltpu.VMEM((width, cols), jnp.bfloat16),
            pltpu.VMEM((width, cols), jnp.bfloat16),
            pltpu.VMEM((BLK, cols), jnp.float32),
        ],
    )
    return pl.pallas_call(
        child_schur_kernel,
        grid_spec=grid_spec,
        out_shape=jax.ShapeDtypeStruct(
            (row_count, cap_cols, cap_rows, BLK, col_count * BLK), jnp.float32
        ),
        compiler_params=params(),
        name="child_schur",
    )(row_pick.reshape(-1), col_pick.reshape(-1), front, rows_factor, cols_factor)


def parent_schur_kernel(starts, front_ref, rows_ref, cols_ref, out_ref, cols_head, cols_tail):
    step = pl.program_id(0)

    @pl.when(step == 0)
    def _():
        cols_head[...], cols_tail[...] = split_parts(cols_ref[...])

    width = cols_ref.shape[0]
    shape = out_ref.shape
    row_ids = starts[0] + step * shape[0] + lax.broadcasted_iota(jnp.int32, (shape[0], 1), 0)
    col_ids = starts[1] + lax.broadcasted_iota(jnp.int32, (1, shape[1]), 1)
    update = three_dots(rows_ref[...], cols_head[...], cols_tail[...])
    keep = (row_ids >= width) & (col_ids >= width)
    out_ref[...] = jnp.where(keep, front_ref[...] - update, 0.0)


def parent_schur_of(front, rows_factor, cols_factor, starts):
    rows, cols = front.shape
    width = cols_factor.shape[0]
    tile = 2 * BLK
    grid_spec = pltpu.PrefetchScalarGridSpec(
        num_scalar_prefetch=1,
        grid=(rows // tile,),
        in_specs=[
            pl.BlockSpec((tile, cols), lambda i, s: (i, 0)),
            pl.BlockSpec((tile, width), lambda i, s: (i, 0)),
            pl.BlockSpec((width, cols), lambda i, s: (0, 0)),
        ],
        out_specs=pl.BlockSpec((tile, cols), lambda i, s: (i, 0)),
        scratch_shapes=[
            pltpu.VMEM((width, cols), jnp.bfloat16),
            pltpu.VMEM((width, cols), jnp.bfloat16),
        ],
    )
    return pl.pallas_call(
        parent_schur_kernel,
        grid_spec=grid_spec,
        out_shape=jax.ShapeDtypeStruct((rows, cols), jnp.float32),
        compiler_params=params(),
        name="parent_schur",
    )(starts, front, rows_factor, cols_factor)


def squeeze_kernel(source, *refs):
    ins, out_ref = refs[:-1], refs[-1]
    step = pl.program_id(0)
    for t, ref in enumerate(ins):

        @pl.when(source[2 * step] == t)
        def _(ref=ref):
            for e in range(out_ref.shape[0]):
                out_ref[e, 0] = ref[0, :, e * BLK : (e + 1) * BLK]


def squeeze_rows(parts, source):
    incoming = source.shape[0]
    cols = parts[0].shape[2]
    count = cols // BLK
    grid_spec = pltpu.PrefetchScalarGridSpec(
        num_scalar_prefetch=1,
        grid=(incoming,),
        in_specs=[pl.BlockSpec((1, BLK, cols), lambda m, s: (s[2 * m + 1], 0, 0)) for _ in parts],
        out_specs=pl.BlockSpec((count, 1, BLK, BLK), lambda m, s: (0, m, 0, 0)),
    )
    return pl.pallas_call(
        squeeze_kernel,
        grid_spec=grid_spec,
        out_shape=jax.ShapeDtypeStruct((count, incoming, BLK, BLK), jnp.float32),
        compiler_params=params(),
        name="squeeze_rows",
    )(source.reshape(-1), *parts)


def extend_add_kernel(cap_cols, row_from, col_from, front_ref, *refs):
    pieces, out_ref = refs[:-1], refs[-1]
    step = pl.program_id(0)
    span = out_ref.shape[1] // BLK
    for y in range(span):
        lanes = slice(y * BLK, (y + 1) * BLK)
        total = front_ref[:, lanes].astype(jnp.float32)
        for child in range(2):
            valid_row = row_from[child * pl.num_programs(0) + step] >= 0
            for j in range(cap_cols):
                place = col_from[(child * cap_cols + j) * span + y]
                tile = pieces[child * cap_cols + j][jnp.maximum(place, 0), 0]
                total = total + jnp.where(valid_row & (place >= 0), tile, 0.0)
        out_ref[:, lanes] = total


def extend_add(front, pieces, row_from, col_from):
    rows, cols = front.shape
    cap_cols = col_from.shape[1]
    blocks = rows // BLK
    count = pieces[0].shape[0]

    def piece_spec(child):
        return pl.BlockSpec(
            (count, 1, BLK, BLK),
            lambda x, rf, cf: (0, jnp.maximum(rf[child * blocks + x], 0), 0, 0),
        )

    grid_spec = pltpu.PrefetchScalarGridSpec(
        num_scalar_prefetch=2,
        grid=(blocks,),
        in_specs=[pl.BlockSpec((BLK, cols), lambda x, rf, cf: (x, 0))]
        + [piece_spec(child) for child in range(2) for _ in range(cap_cols)],
        out_specs=pl.BlockSpec((BLK, cols), lambda x, rf, cf: (x, 0)),
    )
    return pl.pallas_call(
        functools.partial(extend_add_kernel, cap_cols),
        grid_spec=grid_spec,
        out_shape=jax.ShapeDtypeStruct((rows, cols), jnp.float32),
        compiler_params=params(),
        name="extend_add",
    )(row_from.reshape(-1), col_from.reshape(-1), front, *pieces)


def find(match, values, missing):
    found = jnp.sum(jnp.where(match, values, 0), axis=-1)
    return jnp.where(jnp.any(match, axis=-1), found, missing).astype(jnp.int32)


def ranks(group):
    ids = jnp.arange(group.shape[0])
    earlier = ids[None, :] < ids[:, None]
    return jnp.sum(earlier & (group[None, :] == group[:, None]), axis=1)


def shards(child_front, parent_front, block_map):
    leaf_id = lax.axis_index("leaf")
    row_id = lax.axis_index("row")
    col_id = lax.axis_index("col")
    row_count = lax.axis_size("row")
    col_count = lax.axis_size("col")
    own_half = leaf_id % 2

    child_block = child_front[0]
    child_rows, child_cols = child_block.shape
    width = child_cols // 2
    top = from_first_row(child_block[:width])
    slab_head = from_root(child_block[:width, :width], "col", col_id == 0)
    slab_rest, slab_head = lax.optimization_barrier((child_block[width:, :width], slab_head))
    slab_rest = from_root(slab_rest, "col", col_id == 0)
    inverse = inverse_factor_of(from_first_row(slab_head))
    slab = jnp.concatenate((slab_head, slab_rest), axis=0)
    cols_factor = jnp.dot(inverse, top, precision=HIGH)
    rows_factor = jnp.dot(slab, inverse.T, precision=HIGH)
    out_width = width // col_count
    inverse_share = lax.dynamic_slice_in_dim(inverse, col_id * out_width, out_width, 0)
    child_out = lax.dot_general(inverse_share, slab, (((1,), (1,)), ((), ())), precision=HIGH)[None]

    parent_rows, parent_cols = parent_front.shape
    parent_order = parent_rows * row_count
    row_span = parent_rows // BLK
    col_span = parent_cols // BLK
    cap_rows = max(1, child_rows // BLK // row_count)
    cap_cols = max(1, child_cols // BLK // col_count)
    block_count = block_map.shape[1]
    cap_incoming = -(-block_count // row_count)
    global_ids = width + jnp.arange(block_count) * BLK
    src_row = global_ids // child_rows
    src_col = global_ids // child_cols

    def routes(mapping):
        dst_row = mapping // row_span
        owner = mapping // col_span
        rank_row = ranks(src_row * row_count + dst_row)
        rank_col = ranks(src_col * col_count + owner % col_count)
        return dst_row, owner, rank_row, rank_col, ranks(dst_row)

    own_map = lax.dynamic_index_in_dim(block_map, leaf_id, 0, keepdims=False)
    pair_map = lax.dynamic_index_in_dim(block_map, leaf_id ^ 1, 0, keepdims=False)
    dst_row, owner, rank_row, rank_col, rank_dest = routes(own_map)
    distance = jnp.arange(row_count)[:, None, None]
    row_pick = find(
        (src_row == row_id)
        & (dst_row == (row_id + distance) % row_count)
        & (rank_row == jnp.arange(cap_rows)[None, :, None]),
        (global_ids - row_id * child_rows) // BLK,
        0,
    )
    col_pick = find(
        (src_col == col_id)
        & (owner % col_count == jnp.arange(col_count)[:, None, None])
        & (rank_col == jnp.arange(cap_cols)[None, :, None]),
        (global_ids - col_id * child_cols) // BLK,
        0,
    )
    incoming = (dst_row == row_id) & (rank_dest == jnp.arange(cap_incoming)[:, None])
    source = jnp.stack(
        [find(incoming, (row_id - src_row) % row_count, 0), find(incoming, rank_row, 0)], axis=1
    )
    row_from, col_from = [], []
    for mapping in (own_map, pair_map):
        to_row, to_owner, _, to_rank_col, to_rank_dest = routes(mapping)
        row_from.append(
            find(
                (to_row == row_id) & (mapping % row_span == jnp.arange(row_span)[:, None]),
                to_rank_dest,
                -1,
            )
        )
        col_from.append(
            find(
                (to_owner == own_half * col_count + col_id)
                & (mapping % col_span == jnp.arange(col_span)[:, None])
                & (to_rank_col == jnp.arange(cap_cols)[:, None, None]),
                src_col,
                -1,
            )
        )
    row_from = jnp.stack(row_from)
    col_from = jnp.stack(col_from)

    strips = child_strips(child_block, rows_factor, cols_factor, row_pick, col_pick)
    own_pieces, pair_pieces = [], []
    for j in range(cap_cols):
        parts = [strips[0, j]] + [shift_rows(strips[t, j], t) for t in range(1, row_count)]
        sending = squeeze_rows(parts, source)
        landed = lax.all_to_all(
            sending.reshape(col_count, cap_incoming * BLK, BLK),
            "col",
            split_axis=0,
            concat_axis=0,
            tiled=True,
        ).reshape(col_count, cap_incoming, BLK, BLK)
        own_pieces.append(landed)
        pair_pieces.append(pair_swap(landed))
    assembled = extend_add(parent_front, own_pieces + pair_pieces, row_from, col_from)

    parent_width = parent_cols // 2
    parent_top = from_first_row(assembled[:parent_width])
    corner = from_root(assembled[:parent_width, :parent_width], "col", col_id == 0)
    parent_top, corner = lax.optimization_barrier((parent_top, corner))
    corner = from_first_row(jnp.where(own_half == 0, corner, pair_swap(corner)))
    if row_count == 2:
        part = parent_width // 2
        kept = jnp.where(own_half == 0, parent_top[:part], parent_top[part:])
        given = jnp.where(own_half == 0, parent_top[part:], parent_top[:part])
        kept = jnp.where(own_half == row_id, kept, pair_swap(given))
        gathered = lax.all_gather(kept, "col")
        other = pair_swap(gathered)
        first = jnp.where(own_half == 0, gathered, other)
        second = jnp.where(own_half == 0, other, gathered)
        panel_t = jnp.concatenate((first, second), axis=1)
    else:
        panel = from_root(assembled[:, :parent_width], "col", col_id == 0)
        panel = jnp.where(own_half == 0, panel, pair_swap(panel))
        panel_t = panel.T[None]
    parent_inverse = inverse_factor_of(corner)
    parent_cols_factor = jnp.dot(parent_inverse, parent_top, precision=HIGH)
    parent_rows_factor = jnp.einsum("cks,pk->csp", panel_t, parent_inverse, precision=HIGH)
    parent_rows_factor = parent_rows_factor.reshape(parent_rows, parent_width)
    share_width = parent_width // (2 * col_count)
    share_start = (own_half * col_count + col_id) * share_width
    share = lax.dynamic_slice_in_dim(parent_inverse, share_start, share_width, 0)
    parent_out = jnp.einsum("qk,cks->qcs", share, panel_t, precision=HIGH)
    parent_out = parent_out.reshape(share_width, parent_rows)
    col_start = own_half * (parent_order // 2) + col_id * parent_cols
    starts = jnp.stack([row_id * parent_rows, col_start]).astype(jnp.int32)
    parent_schur = parent_schur_of(assembled, parent_rows_factor, parent_cols_factor, starts)
    return (child_out, parent_out, parent_schur)


def solution(mesh):
    placed = (P("leaf", "row", "col"), P("row", ("leaf", "col")), P())
    return jax.shard_map(
        shards,
        mesh=mesh,
        in_specs=placed,
        out_specs=(P("leaf", "col", "row"), P(("leaf", "col"), "row"), P("row", ("leaf", "col"))),
        check_vma=False,
    )
```
